128 devices in a mesh: ops: 8 (over x, core), sec: 16 (over z, y).
Axes of the slice: x: 4, y: 4, z: 4, core: 2. Of those that a mesh axis runs over, the one named last changes fastest.
Arguments:
- psi: float32 [64, 128, 128], P('sec'), may hold values from -20 to 20
- diag_part: float32 [64, 128, 128], P('sec'), may hold values from 1 to 10
- left_ops: bfloat16 [16384, 128, 128], P(('ops', 'sec')), may hold values from -0.09375 to 0.09375
- right_ops: bfloat16 [16384, 128, 128], P(('ops', 'sec')), may hold values from -0.09375 to 0.09375
- source_sec: int32 [16384], P(('ops', 'sec')), may hold values from 0 to 63
- target_sec: int32 [16384, 1], P(('ops', 'sec')), may hold values from 0 to 63; in each aligned block of 128 rows (0 to 127, 128 to 255, ...) at most 4 rows name the same one
Outputs:
- wave_out: float32 [64, 128, 128], P('sec')
The draws below stay inside these ranges and needn't reach their ends.
Inputs may be any that keep to these rules, and one draw needn't show every extreme that they name: `target_sec`: among the pairs of one device, no sector is the target of more than 4 pairs, and in every draw some sector is the target of exactly 4.
All inputs are finite; a program needn't handle non-finite values.
Results may differ from the reference program's by a relative error of at most 0.00055.
Values may be sent and summed in bfloat16 or wider, within the bound.
A program may use at most 128 MiB of HBM per device.

```python
import math
import jax
import jax.numpy as jnp
import numpy as np
from jax import lax

B = 128
PAIRS_DEV = 128
MOST = 4
ITERS = 3
NSEC = 64
PAIRS = 16384


def sector_ramp():
    return (jnp.arange(NSEC, dtype=jnp.float32) / max(NSEC - 1, 1))[:, None, None]


def draw_psi(key, part):
    key = jax.random.fold_in(key, 11)
    ramp = sector_ramp()
    values = jax.random.truncated_normal(key, -6.0, 6.0, (NSEC, B, B), jnp.float32)
    return values * jnp.exp(ramp * math.log(3.0))


def draw_diag_part(key, part):
    key = jax.random.fold_in(key, 12)
    ramp = sector_ramp()
    spread = jax.random.uniform(key, (NSEC, B, B), jnp.float32, 0.0, 1.0)
    place = 0.5 * ramp + 0.5 * spread
    return jnp.exp(place * math.log(10.0))


def set_ends(drawn, stream_key, smallest, high):
    longest = drawn.shape.index(max(drawn.shape))
    spots = []
    for shift in (0, 1):
        where = [jax.random.randint(jax.random.fold_in(stream_key, axis), (), 0, length) for axis, length in enumerate(drawn.shape)]
        where[longest] = (where[longest] + shift) % drawn.shape[longest]
        spots.append(tuple(where))
    return drawn.at[spots[0]].set(smallest).at[spots[1]].set(high)


def shard_levels(key, shape, shards, low, top_value):
    factor_of, own = 1.0, jax.random.fold_in(key, 6)
    for position, shards_of in shards:
        heights = jnp.exp(jax.random.uniform(jax.random.fold_in(own, position), (shards_of,), jnp.float32, low / len(shards), top_value / len(shards)))
        factor_of = factor_of * jnp.repeat(heights, shape[position] // shards_of).reshape([-1 if axis == position else 1 for axis in range(len(shape))])
    return factor_of


def routed_block(rng, own, number, rows, amount, top, bound, lean):
    order = jax.random.permutation(rng, amount)
    heavy_load, usual = shares(amount, rows * top, bound, lean, True), shares(amount, rows * top, bound, lean, False)
    places = jnp.arange(amount)

    def named(sizes, rotation):
        used = int((sizes > 0).sum())
        fixed = max(1, used // 4)
        moved = fixed + (places - fixed + rotation * (used - fixed)) % max(1, amount - fixed)
        return jnp.zeros((amount,), jnp.int32).at[order[jnp.where(places < fixed, places, moved)]].set(jnp.asarray(sizes, jnp.int32))

    sizes = jnp.where(number % 4 == 0, named(heavy_load, number // 4), named(usual, number - number // 4 - 1))
    mixed = jax.random.permutation(jax.random.fold_in(own, 3), amount)
    donor, sink = mixed[0:amount // 2 * 2:2], mixed[1:amount // 2 * 2:2]
    slack = jnp.minimum(sizes[donor] - 1, bound - sizes[sink]) // 2
    slack = jnp.where((donor == order[0]) | (sink == order[0]) | (sizes[sink] == 0), 0, jnp.maximum(slack, 0))
    moved = jax.random.randint(jax.random.fold_in(own, 4), (amount // 2,), 0, 1 << 20) % (slack + 1)
    sizes = sizes.at[donor].add(-moved).at[sink].add(moved)
    items = jnp.searchsorted(jnp.cumsum(sizes), jnp.arange(rows * top), side="right").astype(jnp.int32)
    grid = items.reshape(top, rows).T
    grid = grid[jax.random.permutation(jax.random.fold_in(own, 1), rows)]
    rotation = jax.random.randint(jax.random.fold_in(own, 2), (rows, 1), 0, top)
    return jnp.take_along_axis(grid, (jnp.arange(top)[None, :] + rotation) % top, axis=1)


def shares(count, total, bound, slope, full):
    portions = [(1 << 20) // math.isqrt(standing ** slope) + 1 for standing in range(1, count + 1)]
    largest = bound if full else min(bound, max(-(-total // count), total * portions[0] // sum(portions)))
    least = 1 if total - largest >= count - 1 else 0
    holding, rest = [largest] + [least] * (count - 1), total - largest - least * (count - 1)
    while rest > 0:
        candidates = [i for i in range(1, count) if holding[i] < largest] or [i for i in range(1, count) if holding[i] < bound]
        pool, budget = sum([portions[i] for i in candidates]), rest
        for i in candidates:
            extra = min(bound - holding[i], max(1, budget * portions[i] // pool), rest)
            holding[i] = holding[i] + extra
            rest = rest - extra
    return np.array(holding)


def bell_draw(key, shape, deviation, reach, shards=(), kind=jnp.bfloat16):
    loudness = shard_levels(key, shape, shards, -0.22, 0.18) if shards else 1.0
    entries = jax.random.normal(key, shape, jnp.float32) * deviation * loudness
    return jnp.minimum(jnp.maximum(entries, -reach), reach).astype(kind)


def setup_inputs(seed: int = 0) -> dict:
    seeds = jax.random.split(jax.random.key(seed), 7)
    psi = draw_psi(jax.random.fold_in(seeds[6], 71), 0)
    diag_part = draw_diag_part(jax.random.fold_in(seeds[6], 71), 0)
    left_ops = bell_draw(seeds[2], (PAIRS, B, B), (B * 32) ** -0.5, 0.09375, ((0, 128),))
    right_ops = bell_draw(seeds[3], (PAIRS, B, B), (B * 32) ** -0.5, 0.09375, ((0, 128),))
    source_sec = set_ends(jax.random.randint(seeds[4], (PAIRS,), 0, NSEC), jax.random.fold_in(seeds[4], 1), 0, NSEC - 1).astype(jnp.int32)
    target_sec_keys = jax.random.split(jax.random.fold_in(seeds[5], 1), PAIRS // PAIRS_DEV)
    target_sec_turns = jax.random.permutation(jax.random.fold_in(seeds[5], 3), PAIRS // PAIRS_DEV)
    target_sec = jax.vmap(lambda own, number: routed_block(jax.random.fold_in(seeds[5], 2), own, number, PAIRS_DEV, NSEC, 1, MOST, 1))(target_sec_keys, target_sec_turns).reshape((PAIRS, 1))
    return dict(psi=psi, diag_part=diag_part, left_ops=left_ops, right_ops=right_ops, source_sec=source_sec, target_sec=target_sec)


def pair_sigma(wave, left_ops, right_ops, source_sec, target_sec):
    blocks = left_ops.shape[0] // PAIRS_DEV
    lefts = left_ops.reshape(blocks, PAIRS_DEV, B, B)
    rights = right_ops.reshape(blocks, PAIRS_DEV, B, B)
    sources = source_sec.reshape(blocks, PAIRS_DEV)
    targets = target_sec[:, 0].reshape(blocks, PAIRS_DEV)

    def step_block(total, items):
        left, right, src, tgt = items
        picked = wave[src].astype(jnp.float32)
        half = jnp.einsum('pij,pjk->pik', left.astype(jnp.float32), picked, precision=lax.Precision.HIGHEST).astype(jnp.bfloat16)
        term = jnp.einsum('pik,plk->pil', half.astype(jnp.float32), right.astype(jnp.float32), precision=lax.Precision.HIGHEST)
        return (total + jax.ops.segment_sum(term, tgt, num_segments=NSEC), None)
    start = jnp.zeros((NSEC, B, B), jnp.float32)
    total, _ = lax.scan(step_block, start, (lefts, rights, sources, targets))
    return total

def reference(psi, diag_part, left_ops, right_ops, source_sec, target_sec):
    phi = psi
    for step in range(ITERS):
        wave = phi.astype(jnp.bfloat16)
        sigma = diag_part * phi + pair_sigma(wave, left_ops, right_ops, source_sec, target_sec)
        theta = jnp.sum(phi * sigma) / jnp.sum(phi * phi)
        fresh = phi - (sigma - theta * phi) / (diag_part + 1.0)
        phi = fresh / jnp.sqrt(jnp.mean(fresh * fresh) + 1e-06)
    return phi
```

```python
import jax
import jax.numpy as jnp
from jax import lax
from jax.experimental import pallas as pl
from jax.experimental.pallas import tpu as pltpu
from jax.sharding import PartitionSpec as P

ITERS = 3
MOST = 4
LAG_SEND = 1
LAG_SUM = 6
B = 128
H = 64
PAIRS = 128
NSEC = 64
MESH = pl.DeviceIdType.MESH


def offset(j):
    return 2 - j + 3 * (j // 2) - 2 * (j // 3)


def inverse(d):
    return jnp.where(d == 0, 3, jnp.where(d == 1, 1, jnp.where(d == 2, 0, 2)))


def position():
    o, i = lax.axis_index("ops"), lax.axis_index("sec")
    return o // 2, lax.rem(o, 2), lax.rem(i, 4), i // 4


def column(row):
    return jnp.broadcast_to(row, (B, B)).T


def pair_tables(source, target, x, y, z):
    ids = lax.broadcasted_iota(jnp.int32, (B, B), 1)
    down = lax.broadcasted_iota(jnp.int32, (B, B), 0)
    part = target // 4
    dx = lax.rem(lax.rem(target, 4) - x + 4, 4)
    dy = lax.rem(lax.rem(part, 4) - y + 4, 4)
    dz = lax.rem(part // 4 - z + 4, 4)
    iy, iz = inverse(dy), inverse(dz)
    odd = lax.rem(dx, 2) == 1
    half = jnp.where(odd, 2 * iy + dx // 2, jnp.where(dx == 2, 0, 4) + iz)
    key = (2 * half + jnp.where(odd, 0, 1)) * 4 + jnp.where(odd, iz, iy)
    other = column(key)
    before = (other == key) & (down < ids)

    def count(mask):
        return jnp.sum(jnp.where(mask, 1, 0), axis=0, keepdims=True)

    rank = count(before)
    place = count((other < key) | before)
    place_col = column(place)
    slot_col = column(key * MOST + rank)
    at = place_col == ids

    def pick(mask, values, empty):
        return empty + jnp.sum(jnp.where(mask, values - empty, 0), axis=0, keepdims=True)

    rows = [pick(at, down, 0), pick(at, column(source), 0)]
    for values in (place_col, down):
        for n in range(2):
            rows.append(pick(slot_col == ids + n * B, values, PAIRS))
    return rows


def kernel(
    source_hbm, target_hbm, psi_hbm, diag_hbm, left_hbm, right_hbm, out_ref,
    left, right, half, wave, pown, psend, precv, rsend, rrecv, mid, msum, acc, phi, diag, weight, csum,
    sc_src, sc_d, sc_own, sc_recv, pairs_in, tab_v, tab,
    lsem, g1s, g1r, g2s, g2r, fws, fwr, pss, psr, rss, rsr, mss, msr, dss, dsr, scs, scr, xs, xr, outs, outr, planes,
):
    x, c, y, z = position()
    me = lax.axis_index("ops")
    sec = z * 4 + y
    mine = sec * 4 + x
    rows = pl.ds(c * H, H)
    sibling = (x * 2 + 1 - c, sec)

    loads = [
        pltpu.make_async_copy(source_hbm, pairs_in.at[pl.ds(0, 1)], lsem.at[0]),
        pltpu.make_async_copy(target_hbm, pairs_in.at[pl.ds(1, 1)], lsem.at[1]),
        pltpu.make_async_copy(psi_hbm.at[:, rows], phi, lsem.at[2]),
        pltpu.make_async_copy(diag_hbm.at[:, rows], diag, lsem.at[3]),
        pltpu.make_async_copy(left_hbm, left, lsem.at[4]),
        pltpu.make_async_copy(right_hbm, right.at[pl.ds(0, PAIRS)], lsem.at[5]),
    ]
    for load in loads:
        load.start()

    def chip(k):
        dx, dy, dz = offset(lax.rem(k, 4)), offset(lax.rem(k // 4, 4)), offset(k // 16)
        return chip_at(dx, dy, dz)

    def chip_at(dx, dy, dz):
        return (lax.rem(x + dx, 4) * 2 + c, lax.rem(z + dz, 4) * 4 + lax.rem(y + dy, 4))

    def owner(h, odd):
        if odd:
            return chip_at(2 - 2 * (h // 4), 0, offset(lax.rem(h, 4)))
        return chip_at(1 + 2 * lax.rem(h, 2), offset(h // 2), 0)

    def place(first, second):
        dy = jnp.where(c == 0, first, second)
        dz = jnp.where(c == 0, second, first)
        return lax.rem(z + dz + 4, 4) * 4 + lax.rem(y + dy + 4, 4)

    barrier = pltpu.get_barrier_semaphore()

    for j in range(1, 4):
        for to in (chip_at(j, 0, 0), chip_at(0, j, 0), chip_at(0, 0, j)):
            pl.semaphore_signal(barrier, inc=1, device_id=to, device_id_type=MESH)
    pl.semaphore_signal(barrier, inc=1, device_id=sibling, device_id_type=MESH)

    right[PAIRS] = jnp.zeros((B, B), jnp.bfloat16)
    half[PAIRS] = jnp.zeros((B, B), jnp.bfloat16)
    loads[0].wait()
    loads[1].wait()
    tab_v[...] = jnp.zeros((8, B), jnp.int32)
    for n, row in enumerate(pair_tables(pairs_in[0:1, :], pairs_in[1:2, :], x, y, z)):
        tab_v[n : n + 1, :] = row
    to_scalar = pltpu.make_async_copy(tab_v, tab, lsem.at[6])
    to_scalar.start()
    loads[2].wait()
    own_sectors = pl.ds(sec * 4, 4)
    wave[own_sectors, rows, :] = phi[...].astype(jnp.bfloat16)
    loads[3].wait()
    weight[...] = 1.0 / (diag[...] + 1.0)
    to_scalar.wait()
    pl.semaphore_wait(barrier, 10)

    def remote(src, dst, s, r, to):
        return pltpu.make_async_remote_copy(
            src_ref=src, dst_ref=dst, send_sem=s, recv_sem=r, device_id=to, device_id_type=MESH
        )

    def sectors(at):
        return wave.at[pl.ds(at * 4, 4), rows]

    def first_copy(j):
        return remote(sectors(sec), sectors(sec), g1s.at[j], g1r.at[j], (me, place(j, 0)))

    def second_copy(j, m):
        block = sectors(place(-j, 0))
        n = j * 4 + m
        return remote(block, block, g2s.at[n], g2r.at[n], (me, place(0, m)))

    def forward_copy(j, m):
        block = sectors(place(-j, -m))
        n = j * 4 + m
        return remote(block, block, fws.at[n], fwr.at[n], sibling)

    def partial_copy(b):
        return remote(psend.at[b], precv.at[b], pss.at[b], psr.at[b], sibling)

    def line_sum_copy(h, odd, kk):
        k = (2 * h + odd) * 4 + kk
        j = offset(kk)
        to = chip_at(0, j, 0) if odd else chip_at(0, 0, j)
        return remote(rsend.at[k], rrecv.at[k], rss.at[k], rsr.at[k], to)

    def owner_copy(h, odd):
        g = 2 * h + odd
        return remote(mid.at[g], msum.at[g], mss.at[g], msr.at[g], owner(h, odd))

    def scalar_copy(k):
        return remote(sc_own, sc_recv.at[k], scs.at[k], scr.at[k], chip(k))

    def line_copy(j):
        to = (lax.rem(x + j, 4) * 2 + c, sec)
        return remote(acc, csum.at[x], xs.at[j], xr.at[j], to)

    def left_products(n):
        picked = wave[tab[1, n]]
        half[n] = jnp.dot(left[tab[0, n]], picked, preferred_element_type=jnp.float32).astype(
            jnp.bfloat16
        )

    def slot(table, k, r):
        return tab[table + k // 32, lax.rem(k, 32) * MOST + r]

    def right_products(b):
        for kk in range(4):
            k = b * 4 + kk
            total = None
            for r in range(0, MOST, 2):
                a = jnp.concatenate([half[slot(2, k, r)], half[slot(2, k, r + 1)]], axis=1)
                w = jnp.concatenate([right[slot(4, k, r)], right[slot(4, k, r + 1)]], axis=1)
                term = lax.dot_general(
                    a, w, (((1,), (1,)), ((), ())), preferred_element_type=jnp.float32
                )
                total = term if total is None else total + term
            low, high = total[:H], total[H:]
            pown[b, kk] = jnp.where(c == 0, low, high)
            psend[b, kk] = jnp.where(c == 0, high, low)
        partial_copy(b).start()

    def send_group(h):
        for odd in range(2):
            g = 2 * h + odd
            partial_copy(g).wait()
            for kk in range(3):
                rsend[g * 4 + kk] = (pown[g, kk] + precv[g, kk]).astype(jnp.bfloat16)
                line_sum_copy(h, odd, kk).start()
            mid[g] = pown[g, 3] + precv[g, 3]

    def sum_group(h):
        for odd in range(2):
            g = 2 * h + odd
            for kk in range(3):
                line_sum_copy(h, odd, kk).wait()
            got = [rrecv[g * 4 + kk].astype(jnp.float32) for kk in range(3)]
            mid[g] = (mid[g] + got[0]) + (got[1] + got[2])
            if not (isinstance(h, int) and g == 15):
                owner_copy(h, odd).start()

    def step(t, theta_before):
        far = (2, 1, 3)
        near = (1, 3, 2)
        for j in far:
            first_copy(j).start()
        for m in far:
            second_copy(0, m).start()
        forward_copy(0, 0).start()
        for j in near:
            first_copy(j).wait_recv()
            for m in far:
                second_copy(j, m).start()
            forward_copy(j, 0).start()
        for j in (0, *near):
            for m in near:
                second_copy(j, m).wait_recv()
                forward_copy(j, m).start()
        for j in near:
            first_copy(j).wait_send()
        for j in range(4):
            for m in near:
                second_copy(j, m).wait_send()
        for j in range(4):
            for m in range(4):
                forward_copy(j, m).wait()

        @pl.when(t == 0)
        def _():
            for j in range(1, 4):
                pl.semaphore_signal(planes, inc=1, device_id=chip_at(j, 0, 0), device_id_type=MESH)
            loads[4].wait()
            loads[5].wait()

        def products(h, with_left):
            for odd in range(2):
                g = 2 * h + odd
                if with_left:
                    for n in range(16):
                        left_products(g * 16 + n)
                right_products(g)

        def early(h, carry):
            products(h, True)

            @pl.when(h >= LAG_SEND)
            def _():
                send_group(h - LAG_SEND)

            return carry

        def late(h, carry):
            products(h, False)
            send_group(h - LAG_SEND)

            @pl.when(h >= LAG_SUM)
            def _():
                sum_group(h - LAG_SUM)

            return carry

        lax.fori_loop(0, 4, early, 0)

        @pl.when(t == 0)
        def _():
            pl.semaphore_wait(planes, 3)

        lax.fori_loop(4, 8, late, 0)
        for h in range(8 - LAG_SEND, 8):
            send_group(h)
        for h in range(8 - LAG_SUM, 8):
            sum_group(h)

        total = mid[15]
        for h in range(8):
            for odd in range(2):
                if 2 * h + odd < 15:
                    owner_copy(h, odd).wait()
                    total += msum[2 * h + odd]
        acc[...] = total
        for j in range(1, 4):
            line_copy(j).start()

        now = phi[x]
        csum[x] = total
        sigma = diag[x] * now + total
        ua = now * weight[x]
        fa = now - (sigma - theta_before * now) * weight[x]
        lane = lax.broadcasted_iota(jnp.int32, (1, B), 1)
        row = jnp.zeros((1, B), jnp.float32)
        for j, terms in enumerate((now * sigma, now * now, fa * fa, fa * ua, ua * ua)):
            value = jnp.sum(jnp.sum(terms, axis=0, keepdims=True), axis=1, keepdims=True)
            row = jnp.where(lane == j, value, row)
        sc_src[...] = row
        swap = remote(sc_src, sc_d, dss.at[0], dsr.at[0], sibling)
        swap.start()
        swap.wait()
        sc_own[...] = row + sc_d[...]

        def send_scalars(k, carry):
            scalar_copy(k).start()
            return carry

        def wait_scalars(k, carry):
            scalar_copy(k).wait()
            return carry

        lax.fori_loop(0, NSEC - 1, send_scalars, 0)
        sc_recv[NSEC - 1] = sc_own[...]
        lax.fori_loop(0, NSEC - 1, wait_scalars, 0)
        sums = jnp.sum(sc_recv[...], axis=0)
        theta = sums[:, 0:1] / sums[:, 1:2]
        delta = theta - theta_before
        squares = sums[:, 2:3] + delta * (2.0 * sums[:, 3:4] + delta * sums[:, 4:5])
        scale = 1.0 / jnp.sqrt(squares / float(NSEC * B * B) + 1e-06)
        for j in range(1, 4):
            line_copy(j).wait()
        for j in range(4):
            now = phi[j]
            fresh = now - (diag[j] * now + csum[j] - theta * now) * weight[j]
            new = fresh * scale
            phi[j] = new
            wave[sec * 4 + j, rows, :] = new.astype(jnp.bfloat16)
        return theta

    lax.fori_loop(0, ITERS, step, jnp.zeros((1, 1), jnp.float32))

    out_ref[:, rows, :] = phi[...]
    last = remote(phi, out_ref.at[:, rows], outs.at[0], outr.at[0], sibling)
    last.start()
    last.wait()


def shards(psi, diag_part, left_ops, right_ops, source_sec, target_sec):
    vmem = pl.BlockSpec(memory_space=pltpu.VMEM)
    hbm = pl.BlockSpec(memory_space=pl.ANY)
    f32, bf16 = jnp.float32, jnp.bfloat16
    dma = pltpu.SemaphoreType.DMA
    quarter = pltpu.VMEM((4, H, B), f32)
    line = pltpu.VMEM((1, B), f32)
    partial = pltpu.VMEM((16, 4, H, B), f32)
    packed = pltpu.VMEM((NSEC, H, B), bf16)
    return pl.pallas_call(
        kernel,
        out_shape=jax.ShapeDtypeStruct((4, B, B), f32),
        in_specs=[hbm] * 6,
        out_specs=vmem,
        scratch_shapes=[
            pltpu.VMEM((PAIRS, B, B), bf16),
            pltpu.VMEM((PAIRS + 1, B, B), bf16),
            pltpu.VMEM((PAIRS + 1, B, B), bf16),
            pltpu.VMEM((NSEC, B, B), bf16),
            partial,
            partial,
            partial,
            packed,
            packed,
            pltpu.VMEM((16, H, B), f32),
            pltpu.VMEM((16, H, B), f32),
            pltpu.VMEM((H, B), f32),
            quarter,
            quarter,
            quarter,
            quarter,
            line,
            line,
            line,
            pltpu.VMEM((NSEC, 1, B), f32),
            pltpu.VMEM((8, B), jnp.int32),
            pltpu.VMEM((8, B), jnp.int32),
            pltpu.SMEM((8, B), jnp.int32),
            dma((7,)),
            dma((4,)),
            dma((4,)),
            dma((16,)),
            dma((16,)),
            dma((16,)),
            dma((16,)),
            dma((16,)),
            dma((16,)),
            dma((NSEC,)),
            dma((NSEC,)),
            dma((16,)),
            dma((16,)),
            dma((1,)),
            dma((1,)),
            dma((NSEC,)),
            dma((NSEC,)),
            dma((4,)),
            dma((4,)),
            dma((1,)),
            dma((1,)),
            pltpu.SemaphoreType.REGULAR,
        ],
        compiler_params=pltpu.CompilerParams(
            collective_id=0, has_side_effects=True, vmem_limit_bytes=62 << 20
        ),
        cost_estimate=pl.CostEstimate(
            flops=ITERS * PAIRS * 4 * B * B * B, bytes_accessed=9 << 20, transcendentals=0
        ),
        name="davidson",
    )(
        source_sec.reshape(1, PAIRS), target_sec.reshape(1, PAIRS), psi, diag_part, left_ops,
        right_ops,
    )


def solution(mesh):
    placed = (
        P("sec", None, None),
        P("sec", None, None),
        P(("ops", "sec"), None, None),
        P(("ops", "sec"), None, None),
        P(("ops", "sec")),
        P(("ops", "sec"), None),
    )
    return jax.shard_map(
        shards, mesh=mesh, in_specs=placed, out_specs=P("sec", None, None), check_vma=False
    )
```

```python
import jax
import jax.numpy as jnp
from jax import lax
from jax.experimental import pallas as pl
from jax.experimental.pallas import tpu as pltpu
from jax.sharding import PartitionSpec as P

ITERS = 3
MOST = 4
TURNS, EACH = 8, 8
GROUPS = 8
B = 128
H = 64
PAIRS = 128
NSEC = 64
MESH = pl.DeviceIdType.MESH


ORDER = [
    42, 38, 46, 34, 41, 25, 57, 9, 26, 22, 30, 18, 43, 27, 59, 11,
    58, 54, 62, 50, 37, 21, 53, 5, 10, 6, 14, 2, 40, 24, 56, 8,
    39, 45, 47, 23, 61, 29, 55, 31, 63, 33, 36, 35, 44, 7, 13, 15,
    17, 52, 20, 49, 19, 60, 28, 51, 32, 1, 4, 3, 12, 16, 48, 0,
]
WORDS = [
    sum(place * NSEC**n for n, place in enumerate(ORDER[at : at + 5])) for at in range(0, NSEC, 5)
]


def place_of(k):
    word = jnp.int32(WORDS[0])
    for n in range(1, len(WORDS)):
        word = jnp.where(k // 5 == n, jnp.int32(WORDS[n]), word)
    scale = jnp.int32(1)
    for n in range(1, 5):
        scale = jnp.where(lax.rem(k, 5) == n, jnp.int32(NSEC**n), scale)
    return lax.rem(word // scale, NSEC)


def position():
    o, i = lax.axis_index("ops"), lax.axis_index("sec")
    return o // 2, lax.rem(o, 2), lax.rem(i, 4), i // 4


def column(row):
    return jnp.broadcast_to(row, (B, B)).T


def pair_tables(source, target, x, y, z):
    ids = lax.broadcasted_iota(jnp.int32, (B, B), 1)
    down = lax.broadcasted_iota(jnp.int32, (B, B), 0)
    part = target // 4
    dx = lax.rem(lax.rem(target, 4) - x + 4, 4)
    dy = lax.rem(lax.rem(part, 4) - y + 4, 4)
    dz = lax.rem(part // 4 - z + 4, 4)
    seen = dx + 4 * dy + 16 * dz
    key = jnp.zeros_like(seen)
    for n, at in enumerate(ORDER):
        key = jnp.where(seen == at, n, key)
    other = column(key)
    before = (other == key) & (down < ids)

    def count(mask):
        return jnp.sum(jnp.where(mask, 1, 0), axis=0, keepdims=True)

    rank = count(before)
    place = count((other < key) | before)
    place_col = column(place)
    slot_col = column(key * MOST + rank)
    at = place_col == ids

    def pick(mask, values, empty):
        return empty + jnp.sum(jnp.where(mask, values - empty, 0), axis=0, keepdims=True)

    rows = [pick(at, down, 0), pick(at, column(source), 0)]
    for values in (place_col, down):
        for n in range(2):
            rows.append(pick(slot_col == ids + n * B, values, PAIRS))
    return rows


def kernel(
    source_hbm, target_hbm, psi_hbm, diag_hbm, left_hbm, right_hbm, out_ref,
    left, right, half, wave, pown, psend, precv, rsend, rrecv, mid, msum, acc, phi, diag, weight, csum,
    sc_src, sc_d, sc_own, sc_recv, pairs_in, tab_v, tab,
    lsem, g1s, g1r, g2s, g2r, fws, fwr, pss, psr, rss, rsr, mss, msr, dss, dsr, scs, scr, xs, xr, outs, outr, planes,
):
    x, c, y, z = position()
    me = lax.axis_index("ops")
    sec = z * 4 + y
    mine = sec * 4 + x
    rows = pl.ds(c * H, H)
    sibling = (x * 2 + 1 - c, sec)

    loads = [
        pltpu.make_async_copy(source_hbm, pairs_in.at[pl.ds(0, 1)], lsem.at[0]),
        pltpu.make_async_copy(target_hbm, pairs_in.at[pl.ds(1, 1)], lsem.at[1]),
        pltpu.make_async_copy(psi_hbm.at[:, rows], phi, lsem.at[2]),
        pltpu.make_async_copy(diag_hbm.at[:, rows], diag, lsem.at[3]),
        pltpu.make_async_copy(left_hbm, left, lsem.at[4]),
        pltpu.make_async_copy(right_hbm, right.at[pl.ds(0, PAIRS)], lsem.at[5]),
    ]
    for load in loads:
        load.start()

    def chip(k):
        q = place_of(k)
        return chip_at(lax.rem(q, 4), lax.rem(q // 4, 4), q // 16)

    def chip_at(dx, dy, dz):
        return (lax.rem(x + dx, 4) * 2 + c, lax.rem(z + dz, 4) * 4 + lax.rem(y + dy, 4))

    def place(first, second):
        dy = jnp.where(c == 0, first, second)
        dz = jnp.where(c == 0, second, first)
        return lax.rem(z + dz + 4, 4) * 4 + lax.rem(y + dy + 4, 4)

    barrier = pltpu.get_barrier_semaphore()

    for j in range(1, 4):
        for to in (chip_at(j, 0, 0), chip_at(0, j, 0), chip_at(0, 0, j)):
            pl.semaphore_signal(barrier, inc=1, device_id=to, device_id_type=MESH)
    pl.semaphore_signal(barrier, inc=1, device_id=sibling, device_id_type=MESH)

    loads[2].wait()
    wave[pl.ds(sec * 4, 4), rows, :] = phi[...].astype(jnp.bfloat16)
    pl.semaphore_wait(barrier, 10)

    def remote(src, dst, s, r, to):
        return pltpu.make_async_remote_copy(
            src_ref=src, dst_ref=dst, send_sem=s, recv_sem=r, device_id=to, device_id_type=MESH
        )

    def sectors(at):
        return wave.at[pl.ds(at * 4, 4), rows]

    def first_copy(j):
        return remote(sectors(sec), sectors(sec), g1s.at[j], g1r.at[j], (me, place(j, 0)))

    def second_copy(j, m):
        block = sectors(place(-j, 0))
        n = j * 4 + m
        return remote(block, block, g2s.at[n], g2r.at[n], (me, place(0, m)))

    def forward_copy(j, m):
        block = sectors(place(-j, -m))
        n = j * 4 + m
        return remote(block, block, fws.at[n], fwr.at[n], sibling)

    def partial_copy(b):
        return remote(psend.at[b], precv.at[b], pss.at[b], psr.at[b], sibling)

    def line_sum_copy(g, kk):
        k = g * 4 + kk
        q = place_of(k)
        across = jnp.where(lax.rem(q, 4) == 2, 1, 0)
        to = chip_at(0, across * lax.rem(q // 4, 4), (1 - across) * (q // 16))
        return remote(rsend.at[k], rrecv.at[k], rss.at[k], rsr.at[k], to)

    def plane_sum_copy(g):
        return remote(mid.at[g], msum.at[g], mss.at[g], msr.at[g], chip(g * 4 + 3))

    def sum_copy(k):
        return remote(rsend.at[k], rrecv.at[k], rss.at[k], rsr.at[k], chip(k))

    def scalar_copy(k):
        return remote(sc_own, sc_recv.at[mine], scs.at[k], scr.at[k], chip(k))

    def line_copy(j):
        to = (lax.rem(x + j, 4) * 2 + c, sec)
        return remote(acc, csum.at[x], xs.at[j], xr.at[j], to)

    def left_products(n):
        picked = wave[tab[1, n]]
        half[n] = jnp.dot(left[tab[0, n]], picked, preferred_element_type=jnp.float32).astype(
            jnp.bfloat16
        )

    def slot(table, k, r):
        return tab[table + k // 32, lax.rem(k, 32) * MOST + r]

    def right_products(h):
        for i in range(EACH):
            k = h * EACH + i
            total = None
            for r in range(0, MOST, 2):
                a = jnp.concatenate([half[slot(2, k, r)], half[slot(2, k, r + 1)]], axis=1)
                w = jnp.concatenate([right[slot(4, k, r)], right[slot(4, k, r + 1)]], axis=1)
                term = lax.dot_general(
                    a, w, (((1,), (1,)), ((), ())), preferred_element_type=jnp.float32
                )
                total = term if total is None else total + term
            low, high = total[:H], total[H:]
            pown[h, i] = jnp.where(c == 0, low, high)
            psend[h, i] = jnp.where(c == 0, high, low)
        partial_copy(h).start()

    def send_lines(h):
        partial_copy(h).wait()
        for i in range(EACH):
            both = pown[h, i] + precv[h, i]
            g, kk = 2 * h + i // 4, i % 4
            if kk == 3:
                mid[g] = both
            else:
                rsend[g * 4 + kk] = both.astype(jnp.bfloat16)
                line_sum_copy(g, kk).start()

    def sum_lines(h):
        for n in range(2):
            g = 2 * h + n
            for kk in range(3):
                line_sum_copy(g, kk).wait_recv()
            got = [rrecv[g * 4 + kk].astype(jnp.float32) for kk in range(3)]
            mid[g] = (mid[g] + got[0]) + (got[1] + got[2])
            plane_sum_copy(g).start()

    def send_straight(h):
        partial_copy(h).wait()
        for i in range(EACH):
            both = pown[h, i] + precv[h, i]
            if isinstance(h, int) and h == TURNS - 1 and i == EACH - 1:
                acc[...] = both
            else:
                rsend[h * EACH + i] = both.astype(jnp.bfloat16)
                sum_copy(h * EACH + i).start()

    def prepare():
        right[PAIRS] = jnp.zeros((B, B), jnp.bfloat16)
        half[PAIRS] = jnp.zeros((B, B), jnp.bfloat16)
        loads[0].wait()
        loads[1].wait()
        tab_v[...] = jnp.zeros((8, B), jnp.int32)
        for n, row in enumerate(pair_tables(pairs_in[0:1, :], pairs_in[1:2, :], x, y, z)):
            tab_v[n : n + 1, :] = row
        to_scalar = pltpu.make_async_copy(tab_v, tab, lsem.at[6])
        to_scalar.start()
        loads[3].wait()
        weight[...] = 1.0 / (diag[...] + 1.0)
        to_scalar.wait()

    def scalars_sent(n, carry):
        for m in range(9):
            scalar_copy(n * 9 + m).wait_send()
        return carry

    def step(t, theta_before):
        far = (2, 1, 3)
        near = (1, 3, 2)
        for j in far:
            first_copy(j).start()
        for m in far:
            second_copy(0, m).start()
        forward_copy(0, 0).start()

        @pl.when(t == 0)
        def _():
            prepare()

        @pl.when(t > 0)
        def _():
            lax.fori_loop(0, 7, scalars_sent, 0)

        for j in near:
            first_copy(j).wait_recv()
            for m in far:
                second_copy(j, m).start()
            forward_copy(j, 0).start()
        for j in (0, *near):
            for m in near:
                second_copy(j, m).wait_recv()
                forward_copy(j, m).start()
        for j in (0, *near):
            for m in (0, *near):
                forward_copy(j, m).wait_recv()

        @pl.when(t == 0)
        def _():
            for j in range(1, 4):
                pl.semaphore_signal(planes, inc=1, device_id=chip_at(j, 0, 0), device_id_type=MESH)
            loads[4].wait()
            loads[5].wait()

        def early(h, carry):
            right_products(h)
            for n in range(32):
                left_products((h + 1) * 32 + n)
            return carry

        def middle(h, carry):
            right_products(h)
            send_lines(h - 2)
            return carry

        def late(h, carry):
            right_products(h)
            send_straight(h - 2)
            return carry

        for n in range(32):
            left_products(n)
        lax.fori_loop(0, 3, early, 0)
        send_lines(0)
        lax.fori_loop(3, 6, middle, 0)

        @pl.when(t == 0)
        def _():
            pl.semaphore_wait(planes, 3)

        lax.fori_loop(6, TURNS, late, 0)
        sum_lines(0)
        send_straight(TURNS - 2)
        sum_lines(1)
        send_straight(TURNS - 1)
        sum_lines(2)
        sum_lines(3)

        for j in (0, *near):
            if j:
                first_copy(j).wait_send()
            for m in (0, *near):
                if m:
                    second_copy(j, m).wait_send()
                forward_copy(j, m).wait_send()

        def collect(n, carry):
            got = []
            for m in range(8):
                k = GROUPS * 4 + n * 8 + m
                sum_copy(k).wait_recv()
                got.append(rrecv[k].astype(jnp.float32))
            pairs = [got[m] + got[m + 1] for m in range(0, 8, 2)]
            acc[...] += (pairs[0] + pairs[1]) + (pairs[2] + pairs[3])
            return carry

        lax.fori_loop(0, 3, collect, 0)
        total = acc[...]
        for k in range(NSEC - 8, NSEC - 1):
            sum_copy(k).wait_recv()
            total += rrecv[k].astype(jnp.float32)
        for g in range(GROUPS):
            plane_sum_copy(g).wait_recv()
            total += msum[g]
        acc[...] = total
        for j in range(1, 4):
            line_copy(j).start()

        now = phi[x]
        csum[x] = total
        sigma = diag[x] * now + total
        ua = now * weight[x]
        fa = now - (sigma - theta_before * now) * weight[x]
        lane = lax.broadcasted_iota(jnp.int32, (1, B), 1)
        row = jnp.zeros((1, B), jnp.float32)
        for j, terms in enumerate((now * sigma, now * now, fa * fa, fa * ua, ua * ua)):
            value = jnp.sum(jnp.sum(terms, axis=0, keepdims=True), axis=1, keepdims=True)
            row = jnp.where(lane == j, value, row)
        sc_src[...] = row
        swap = remote(sc_src, sc_d, dss.at[0], dsr.at[0], sibling)
        swap.start()
        swap.wait()
        sc_own[...] = row + sc_d[...]

        def send_scalars(n, carry):
            for m in range(9):
                scalar_copy(n * 9 + m).start()
            return carry

        def wait_scalars(n, carry):
            for m in range(9):
                scalar_copy(n * 9 + m).wait_recv()
            return carry

        lax.fori_loop(0, 7, send_scalars, 0)
        sc_recv[mine] = sc_own[...]
        for g in range(GROUPS):
            for kk in range(3):
                line_sum_copy(g, kk).wait_send()
            plane_sum_copy(g).wait_send()
        for k in range(GROUPS * 4, NSEC - 1):
            sum_copy(k).wait_send()
        lax.fori_loop(0, 7, wait_scalars, 0)
        sums = jnp.sum(sc_recv[...], axis=0)
        theta = sums[:, 0:1] / sums[:, 1:2]
        delta = theta - theta_before
        squares = sums[:, 2:3] + delta * (2.0 * sums[:, 3:4] + delta * sums[:, 4:5])
        scale = 1.0 / jnp.sqrt(squares / float(NSEC * B * B) + 1e-06)
        for j in range(1, 4):
            line_copy(j).wait()
        for j in range(4):
            now = phi[j]
            fresh = now - (diag[j] * now + csum[j] - theta * now) * weight[j]
            new = fresh * scale
            phi[j] = new
            wave[sec * 4 + j, rows, :] = new.astype(jnp.bfloat16)
        return theta

    lax.fori_loop(0, ITERS, step, jnp.zeros((1, 1), jnp.float32))
    lax.fori_loop(0, 7, scalars_sent, 0)

    out_ref[:, rows, :] = phi[...]
    last = remote(phi, out_ref.at[:, rows], outs.at[0], outr.at[0], sibling)
    last.start()
    last.wait()


def shards(psi, diag_part, left_ops, right_ops, source_sec, target_sec):
    vmem = pl.BlockSpec(memory_space=pltpu.VMEM)
    hbm = pl.BlockSpec(memory_space=pl.ANY)
    f32, bf16 = jnp.float32, jnp.bfloat16
    dma = pltpu.SemaphoreType.DMA
    quarter = pltpu.VMEM((4, H, B), f32)
    line = pltpu.VMEM((1, B), f32)
    partial = pltpu.VMEM((TURNS, EACH, H, B), f32)
    packed = pltpu.VMEM((NSEC, H, B), bf16)
    return pl.pallas_call(
        kernel,
        out_shape=jax.ShapeDtypeStruct((4, B, B), f32),
        in_specs=[hbm] * 6,
        out_specs=vmem,
        scratch_shapes=[
            pltpu.VMEM((PAIRS, B, B), bf16),
            pltpu.VMEM((PAIRS + 1, B, B), bf16),
            pltpu.VMEM((PAIRS + 1, B, B), bf16),
            pltpu.VMEM((NSEC, B, B), bf16),
            partial,
            partial,
            partial,
            packed,
            packed,
            pltpu.VMEM((GROUPS, H, B), f32),
            pltpu.VMEM((GROUPS, H, B), f32),
            pltpu.VMEM((H, B), f32),
            quarter,
            quarter,
            quarter,
            quarter,
            line,
            line,
            line,
            pltpu.VMEM((NSEC, 1, B), f32),
            pltpu.VMEM((8, B), jnp.int32),
            pltpu.VMEM((8, B), jnp.int32),
            pltpu.SMEM((8, B), jnp.int32),
            dma((7,)),
            dma((4,)),
            dma((4,)),
            dma((16,)),
            dma((16,)),
            dma((16,)),
            dma((16,)),
            dma((16,)),
            dma((16,)),
            dma((NSEC,)),
            dma((NSEC,)),
            dma((GROUPS,)),
            dma((GROUPS,)),
            dma((1,)),
            dma((1,)),
            dma((NSEC,)),
            dma((NSEC,)),
            dma((4,)),
            dma((4,)),
            dma((1,)),
            dma((1,)),
            pltpu.SemaphoreType.REGULAR,
        ],
        compiler_params=pltpu.CompilerParams(
            collective_id=0, has_side_effects=True, vmem_limit_bytes=62 << 20
        ),
        cost_estimate=pl.CostEstimate(
            flops=ITERS * PAIRS * 4 * B * B * B, bytes_accessed=9 << 20, transcendentals=0
        ),
        name="davidson",
    )(
        source_sec.reshape(1, PAIRS), target_sec.reshape(1, PAIRS), psi, diag_part, left_ops,
        right_ops,
    )


def solution(mesh):
    placed = (
        P("sec", None, None),
        P("sec", None, None),
        P(("ops", "sec"), None, None),
        P(("ops", "sec"), None, None),
        P(("ops", "sec")),
        P(("ops", "sec"), None),
    )
    return jax.shard_map(
        shards, mesh=mesh, in_specs=placed, out_specs=P("sec", None, None), check_vma=False
    )
```

```python
import jax
import jax.numpy as jnp
from jax import lax
from jax.experimental import pallas as pl
from jax.experimental.pallas import tpu as pltpu
from jax.sharding import PartitionSpec as P

ITERS = 3
MOST = 4
TURNS, EACH = 8, 8
GROUPS = 8
B = 128
H = 64
PAIRS = 128
NSEC = 64
MESH = pl.DeviceIdType.MESH


ORDER = [
    38, 37, 39, 36, 26, 22, 30, 18, 41, 25, 57, 9, 46, 45, 47, 44,
    58, 54, 62, 50, 43, 27, 59, 11, 34, 33, 35, 32, 10, 6, 14, 2,
    42, 40, 21, 63, 23, 61, 29, 55, 31, 53, 24, 56, 17, 51, 5, 15,
    19, 49, 7, 13, 20, 60, 28, 52, 8, 1, 3, 16, 48, 4, 12, 0,
]
WORDS = [
    sum(place * NSEC**n for n, place in enumerate(ORDER[at : at + 5])) for at in range(0, NSEC, 5)
]


def offset(kk):
    return (2, 1, 3, 0)[kk]


def place_of(k):
    word = jnp.int32(WORDS[0])
    for n in range(1, len(WORDS)):
        word = jnp.where(k // 5 == n, jnp.int32(WORDS[n]), word)
    scale = jnp.int32(1)
    for n in range(1, 5):
        scale = jnp.where(lax.rem(k, 5) == n, jnp.int32(NSEC**n), scale)
    return lax.rem(word // scale, NSEC)


def position():
    o, i = lax.axis_index("ops"), lax.axis_index("sec")
    return o // 2, lax.rem(o, 2), lax.rem(i, 4), i // 4


def column(row):
    return jnp.broadcast_to(row, (B, B)).T


def pair_tables(source, target, x, y, z):
    ids = lax.broadcasted_iota(jnp.int32, (B, B), 1)
    down = lax.broadcasted_iota(jnp.int32, (B, B), 0)
    part = target // 4
    dx = lax.rem(lax.rem(target, 4) - x + 4, 4)
    dy = lax.rem(lax.rem(part, 4) - y + 4, 4)
    dz = lax.rem(part // 4 - z + 4, 4)
    seen = dx + 4 * dy + 16 * dz
    key = jnp.zeros_like(seen)
    for n, at in enumerate(ORDER):
        key = jnp.where(seen == at, n, key)
    other = column(key)
    before = (other == key) & (down < ids)

    def count(mask):
        return jnp.sum(jnp.where(mask, 1, 0), axis=0, keepdims=True)

    rank = count(before)
    place = count((other < key) | before)
    place_col = column(place)
    slot_col = column(key * MOST + rank)
    at = place_col == ids

    def pick(mask, values, empty):
        return empty + jnp.sum(jnp.where(mask, values - empty, 0), axis=0, keepdims=True)

    rows = [pick(at, down, 0), pick(at, column(source), 0)]
    for values in (place_col, down):
        for n in range(2):
            rows.append(pick(slot_col == ids + n * B, values, PAIRS))
    return rows


def kernel(
    source_hbm, target_hbm, psi_hbm, diag_hbm, left_hbm, right_hbm, out_ref,
    left, right, half, wave, pown, psend, precv, rsend, rrecv, mid, msum, acc, phi, diag, weight, csum,
    sc_src, sc_d, sc_own, sc_recv, pairs_in, tab_v, tab,
    lsem, g1s, g1r, g2s, g2r, fws, fwr, pss, psr, rss, rsr, mss, msr, dss, dsr, scs, scr, xs, xr, outs, outr, planes,
):
    x, c, y, z = position()
    me = lax.axis_index("ops")
    sec = z * 4 + y
    mine = sec * 4 + x
    rows = pl.ds(c * H, H)
    sibling = (x * 2 + 1 - c, sec)

    loads = [
        pltpu.make_async_copy(source_hbm, pairs_in.at[pl.ds(0, 1)], lsem.at[0]),
        pltpu.make_async_copy(target_hbm, pairs_in.at[pl.ds(1, 1)], lsem.at[1]),
        pltpu.make_async_copy(psi_hbm.at[:, rows], phi, lsem.at[2]),
        pltpu.make_async_copy(diag_hbm.at[:, rows], diag, lsem.at[3]),
        pltpu.make_async_copy(left_hbm, left, lsem.at[4]),
        pltpu.make_async_copy(right_hbm, right.at[pl.ds(0, PAIRS)], lsem.at[5]),
    ]
    for load in loads:
        load.start()

    def chip(k):
        q = place_of(k)
        return chip_at(lax.rem(q, 4), lax.rem(q // 4, 4), q // 16)

    def chip_at(dx, dy, dz):
        return (lax.rem(x + dx, 4) * 2 + c, lax.rem(z + dz, 4) * 4 + lax.rem(y + dy, 4))

    def place(first, second):
        dy = jnp.where(c == 0, first, second)
        dz = jnp.where(c == 0, second, first)
        return lax.rem(z + dz + 4, 4) * 4 + lax.rem(y + dy + 4, 4)

    barrier = pltpu.get_barrier_semaphore()

    for j in range(1, 4):
        for to in (chip_at(j, 0, 0), chip_at(0, j, 0), chip_at(0, 0, j)):
            pl.semaphore_signal(barrier, inc=1, device_id=to, device_id_type=MESH)
    pl.semaphore_signal(barrier, inc=1, device_id=sibling, device_id_type=MESH)

    loads[2].wait()
    wave[pl.ds(sec * 4, 4), rows, :] = phi[...].astype(jnp.bfloat16)
    pl.semaphore_wait(barrier, 10)

    def remote(src, dst, s, r, to):
        return pltpu.make_async_remote_copy(
            src_ref=src, dst_ref=dst, send_sem=s, recv_sem=r, device_id=to, device_id_type=MESH
        )

    def sectors(at):
        return wave.at[pl.ds(at * 4, 4), rows]

    def first_copy(j):
        return remote(sectors(sec), sectors(sec), g1s.at[j], g1r.at[j], (me, place(j, 0)))

    def second_copy(j, m):
        block = sectors(place(-j, 0))
        n = j * 4 + m
        return remote(block, block, g2s.at[n], g2r.at[n], (me, place(0, m)))

    def forward_copy(j, m):
        block = sectors(place(-j, -m))
        n = j * 4 + m
        return remote(block, block, fws.at[n], fwr.at[n], sibling)

    def partial_copy(b):
        return remote(psend.at[b], precv.at[b], pss.at[b], psr.at[b], sibling)

    def line_sum_copy(g, kk):
        k = g * 4 + kk
        axis = lax.rem(g, 3)
        to = chip_at(*(jnp.where(axis == n, offset(kk), 0) for n in range(3)))
        return remote(rsend.at[k], rrecv.at[k], rss.at[k], rsr.at[k], to)

    def plane_sum_copy(g):
        return remote(mid.at[g], msum.at[g], mss.at[g], msr.at[g], chip(g * 4 + 3))

    def sum_copy(k):
        return remote(rsend.at[k], rrecv.at[k], rss.at[k], rsr.at[k], chip(k))

    def scalar_copy(k):
        return remote(sc_own, sc_recv.at[mine], scs.at[k], scr.at[k], chip(k))

    def line_copy(j):
        to = (lax.rem(x + j, 4) * 2 + c, sec)
        return remote(acc, csum.at[x], xs.at[j], xr.at[j], to)

    def left_products(n):
        picked = wave[tab[1, n]]
        half[n] = jnp.dot(left[tab[0, n]], picked, preferred_element_type=jnp.float32).astype(
            jnp.bfloat16
        )

    def slot(table, k, r):
        return tab[table + k // 32, lax.rem(k, 32) * MOST + r]

    def right_products(h):
        for i in range(EACH):
            k = h * EACH + i
            total = None
            for r in range(0, MOST, 2):
                a = jnp.concatenate([half[slot(2, k, r)], half[slot(2, k, r + 1)]], axis=1)
                w = jnp.concatenate([right[slot(4, k, r)], right[slot(4, k, r + 1)]], axis=1)
                term = lax.dot_general(
                    a, w, (((1,), (1,)), ((), ())), preferred_element_type=jnp.float32
                )
                total = term if total is None else total + term
            low, high = total[:H], total[H:]
            pown[h, i] = jnp.where(c == 0, low, high)
            psend[h, i] = jnp.where(c == 0, high, low)
        partial_copy(h).start()

    def send_lines(h):
        partial_copy(h).wait()
        for i in range(EACH):
            both = pown[h, i] + precv[h, i]
            g, kk = 2 * h + i // 4, i % 4
            if kk == 3:
                mid[g] = both
            else:
                rsend[g * 4 + kk] = both.astype(jnp.bfloat16)
                line_sum_copy(g, kk).start()

    def sum_lines(h):
        for n in range(2):
            g = 2 * h + n
            for kk in range(3):
                line_sum_copy(g, kk).wait_recv()
            got = [rrecv[g * 4 + kk].astype(jnp.float32) for kk in range(3)]
            mid[g] = (mid[g] + got[0]) + (got[1] + got[2])
            plane_sum_copy(g).start()

    def send_straight(h):
        partial_copy(h).wait()
        for i in range(EACH):
            both = pown[h, i] + precv[h, i]
            if isinstance(h, int) and h == TURNS - 1 and i == EACH - 1:
                acc[...] = both
            else:
                rsend[h * EACH + i] = both.astype(jnp.bfloat16)
                sum_copy(h * EACH + i).start()

    def prepare():
        right[PAIRS] = jnp.zeros((B, B), jnp.bfloat16)
        half[PAIRS] = jnp.zeros((B, B), jnp.bfloat16)
        loads[0].wait()
        loads[1].wait()
        tab_v[...] = jnp.zeros((8, B), jnp.int32)
        for n, row in enumerate(pair_tables(pairs_in[0:1, :], pairs_in[1:2, :], x, y, z)):
            tab_v[n : n + 1, :] = row
        to_scalar = pltpu.make_async_copy(tab_v, tab, lsem.at[6])
        to_scalar.start()
        loads[3].wait()
        weight[...] = 1.0 / (diag[...] + 1.0)
        to_scalar.wait()

    def scalars_sent(n, carry):
        for m in range(9):
            scalar_copy(n * 9 + m).wait_send()
        return carry

    def step(t, theta_before):
        far = (2, 1, 3)
        near = (1, 3, 2)
        for j in far:
            first_copy(j).start()
        for m in far:
            second_copy(0, m).start()
        forward_copy(0, 0).start()

        @pl.when(t == 0)
        def _():
            prepare()

        @pl.when(t > 0)
        def _():
            lax.fori_loop(0, 7, scalars_sent, 0)

        for j in near:
            first_copy(j).wait_recv()
            for m in far:
                second_copy(j, m).start()
            forward_copy(j, 0).start()
        for j in (0, *near):
            for m in near:
                second_copy(j, m).wait_recv()
                forward_copy(j, m).start()
        for j in (0, *near):
            for m in (0, *near):
                forward_copy(j, m).wait_recv()

        @pl.when(t == 0)
        def _():
            for j in range(1, 4):
                pl.semaphore_signal(planes, inc=1, device_id=chip_at(j, 0, 0), device_id_type=MESH)
            loads[4].wait()
            loads[5].wait()

        def early(h, carry):
            right_products(h)
            for n in range(32):
                left_products((h + 1) * 32 + n)
            return carry

        def middle(h, carry):
            right_products(h)
            send_lines(h - 2)
            return carry

        def late(h, carry):
            right_products(h)
            send_straight(h - 2)
            return carry

        for n in range(32):
            left_products(n)
        lax.fori_loop(0, 3, early, 0)
        send_lines(0)
        lax.fori_loop(3, 6, middle, 0)

        @pl.when(t == 0)
        def _():
            pl.semaphore_wait(planes, 3)

        lax.fori_loop(6, TURNS, late, 0)
        sum_lines(0)
        send_straight(TURNS - 2)
        sum_lines(1)
        send_straight(TURNS - 1)
        sum_lines(2)
        sum_lines(3)

        for j in (0, *near):
            if j:
                first_copy(j).wait_send()
            for m in (0, *near):
                if m:
                    second_copy(j, m).wait_send()
                forward_copy(j, m).wait_send()

        def collect(n, carry):
            got = []
            for m in range(8):
                k = GROUPS * 4 + n * 8 + m
                sum_copy(k).wait_recv()
                got.append(rrecv[k].astype(jnp.float32))
            pairs = [got[m] + got[m + 1] for m in range(0, 8, 2)]
            acc[...] += (pairs[0] + pairs[1]) + (pairs[2] + pairs[3])
            return carry

        lax.fori_loop(0, 3, collect, 0)
        total = acc[...]
        for k in range(NSEC - 8, NSEC - 1):
            sum_copy(k).wait_recv()
            total += rrecv[k].astype(jnp.float32)
        for g in range(GROUPS):
            plane_sum_copy(g).wait_recv()
            total += msum[g]
        acc[...] = total
        for j in range(1, 4):
            line_copy(j).start()

        now = phi[x]
        csum[x] = total
        sigma = diag[x] * now + total
        ua = now * weight[x]
        fa = now - (sigma - theta_before * now) * weight[x]
        lane = lax.broadcasted_iota(jnp.int32, (1, B), 1)
        row = jnp.zeros((1, B), jnp.float32)
        for j, terms in enumerate((now * sigma, now * now, fa * fa, fa * ua, ua * ua)):
            value = jnp.sum(jnp.sum(terms, axis=0, keepdims=True), axis=1, keepdims=True)
            row = jnp.where(lane == j, value, row)
        sc_src[...] = row
        swap = remote(sc_src, sc_d, dss.at[0], dsr.at[0], sibling)
        swap.start()
        swap.wait()
        sc_own[...] = row + sc_d[...]

        def send_scalars(n, carry):
            for m in range(9):
                scalar_copy(n * 9 + m).start()
            return carry

        def wait_scalars(n, carry):
            for m in range(9):
                scalar_copy(n * 9 + m).wait_recv()
            return carry

        lax.fori_loop(0, 7, send_scalars, 0)
        sc_recv[mine] = sc_own[...]
        for g in range(GROUPS):
            for kk in range(3):
                line_sum_copy(g, kk).wait_send()
            plane_sum_copy(g).wait_send()
        for k in range(GROUPS * 4, NSEC - 1):
            sum_copy(k).wait_send()
        lax.fori_loop(0, 7, wait_scalars, 0)
        sums = jnp.sum(sc_recv[...], axis=0)
        theta = sums[:, 0:1] / sums[:, 1:2]
        delta = theta - theta_before
        squares = sums[:, 2:3] + delta * (2.0 * sums[:, 3:4] + delta * sums[:, 4:5])
        scale = 1.0 / jnp.sqrt(squares / float(NSEC * B * B) + 1e-06)
        for j in range(1, 4):
            line_copy(j).wait()
        for j in range(4):
            now = phi[j]
            fresh = now - (diag[j] * now + csum[j] - theta * now) * weight[j]
            new = fresh * scale
            phi[j] = new
            wave[sec * 4 + j, rows, :] = new.astype(jnp.bfloat16)
        return theta

    lax.fori_loop(0, ITERS, step, jnp.zeros((1, 1), jnp.float32))
    lax.fori_loop(0, 7, scalars_sent, 0)

    out_ref[:, rows, :] = phi[...]
    last = remote(phi, out_ref.at[:, rows], outs.at[0], outr.at[0], sibling)
    last.start()
    last.wait()


def shards(psi, diag_part, left_ops, right_ops, source_sec, target_sec):
    vmem = pl.BlockSpec(memory_space=pltpu.VMEM)
    hbm = pl.BlockSpec(memory_space=pl.ANY)
    f32, bf16 = jnp.float32, jnp.bfloat16
    dma = pltpu.SemaphoreType.DMA
    quarter = pltpu.VMEM((4, H, B), f32)
    line = pltpu.VMEM((1, B), f32)
    partial = pltpu.VMEM((TURNS, EACH, H, B), f32)
    packed = pltpu.VMEM((NSEC, H, B), bf16)
    return pl.pallas_call(
        kernel,
        out_shape=jax.ShapeDtypeStruct((4, B, B), f32),
        in_specs=[hbm] * 6,
        out_specs=vmem,
        scratch_shapes=[
            pltpu.VMEM((PAIRS, B, B), bf16),
            pltpu.VMEM((PAIRS + 1, B, B), bf16),
            pltpu.VMEM((PAIRS + 1, B, B), bf16),
            pltpu.VMEM((NSEC, B, B), bf16),
            partial,
            partial,
            partial,
            packed,
            packed,
            pltpu.VMEM((GROUPS, H, B), f32),
            pltpu.VMEM((GROUPS, H, B), f32),
            pltpu.VMEM((H, B), f32),
            quarter,
            quarter,
            quarter,
            quarter,
            line,
            line,
            line,
            pltpu.VMEM((NSEC, 1, B), f32),
            pltpu.VMEM((8, B), jnp.int32),
            pltpu.VMEM((8, B), jnp.int32),
            pltpu.SMEM((8, B), jnp.int32),
            dma((7,)),
            dma((4,)),
            dma((4,)),
            dma((16,)),
            dma((16,)),
            dma((16,)),
            dma((16,)),
            dma((16,)),
            dma((16,)),
            dma((NSEC,)),
            dma((NSEC,)),
            dma((GROUPS,)),
            dma((GROUPS,)),
            dma((1,)),
            dma((1,)),
            dma((NSEC,)),
            dma((NSEC,)),
            dma((4,)),
            dma((4,)),
            dma((1,)),
            dma((1,)),
            pltpu.SemaphoreType.REGULAR,
        ],
        compiler_params=pltpu.CompilerParams(
            collective_id=0, has_side_effects=True, vmem_limit_bytes=62 << 20
        ),
        cost_estimate=pl.CostEstimate(
            flops=ITERS * PAIRS * 4 * B * B * B, bytes_accessed=9 << 20, transcendentals=0
        ),
        name="davidson",
    )(
        source_sec.reshape(1, PAIRS), target_sec.reshape(1, PAIRS), psi, diag_part, left_ops,
        right_ops,
    )


def solution(mesh):
    placed = (
        P("sec", None, None),
        P("sec", None, None),
        P(("ops", "sec"), None, None),
        P(("ops", "sec"), None, None),
        P(("ops", "sec")),
        P(("ops", "sec"), None),
    )
    return jax.shard_map(
        shards, mesh=mesh, in_specs=placed, out_specs=P("sec", None, None), check_vma=False
    )
```

```python
import jax
import jax.numpy as jnp
from jax import lax
from jax.experimental import pallas as pl
from jax.experimental.pallas import tpu as pltpu
from jax.sharding import PartitionSpec as P

ITERS = 3
MOST = 4
TURNS, EACH = 8, 8
GROUPS = 8
SHARED = (0, 1)
WHOLE = tuple(j for j in (0, 1, 3, 2) if j not in SHARED)
B = 128
H = 64
PAIRS = 128
NSEC = 64
MESH = pl.DeviceIdType.MESH


ORDER = [
    38, 37, 39, 36, 26, 22, 30, 18, 41, 25, 57, 9, 46, 45, 47, 44,
    58, 54, 62, 50, 43, 27, 59, 11, 34, 33, 35, 32, 10, 6, 14, 2,
    42, 40, 21, 63, 23, 61, 29, 55, 31, 53, 24, 56, 17, 51, 5, 15,
    19, 49, 7, 13, 20, 60, 28, 52, 8, 1, 3, 16, 48, 4, 12, 0,
]
WORDS = [
    sum(place * NSEC**n for n, place in enumerate(ORDER[at : at + 5])) for at in range(0, NSEC, 5)
]


def offset(kk):
    return (2, 1, 3, 0)[kk]


def place_of(k):
    word = jnp.int32(WORDS[0])
    for n in range(1, len(WORDS)):
        word = jnp.where(k // 5 == n, jnp.int32(WORDS[n]), word)
    scale = jnp.int32(1)
    for n in range(1, 5):
        scale = jnp.where(lax.rem(k, 5) == n, jnp.int32(NSEC**n), scale)
    return lax.rem(word // scale, NSEC)


def position():
    o, i = lax.axis_index("ops"), lax.axis_index("sec")
    return o // 2, lax.rem(o, 2), lax.rem(i, 4), i // 4


def column(row):
    return jnp.broadcast_to(row, (B, B)).T


def pair_tables(source, target, x, y, z):
    ids = lax.broadcasted_iota(jnp.int32, (B, B), 1)
    down = lax.broadcasted_iota(jnp.int32, (B, B), 0)
    part = target // 4
    dx = lax.rem(lax.rem(target, 4) - x + 4, 4)
    dy = lax.rem(lax.rem(part, 4) - y + 4, 4)
    dz = lax.rem(part // 4 - z + 4, 4)
    seen = dx + 4 * dy + 16 * dz
    key = jnp.zeros_like(seen)
    for n, at in enumerate(ORDER):
        key = jnp.where(seen == at, n, key)
    other = column(key)
    before = (other == key) & (down < ids)

    def count(mask):
        return jnp.sum(jnp.where(mask, 1, 0), axis=0, keepdims=True)

    rank = count(before)
    place = count((other < key) | before)
    place_col = column(place)
    slot_col = column(key * MOST + rank)
    at = place_col == ids

    def pick(mask, values, empty):
        return empty + jnp.sum(jnp.where(mask, values - empty, 0), axis=0, keepdims=True)

    rows = [pick(at, down, 0), pick(at, column(source), 0)]
    for values in (place_col, down):
        for n in range(2):
            rows.append(pick(slot_col == ids + n * B, values, PAIRS))
    return rows


def kernel(
    source_hbm, target_hbm, psi_hbm, diag_hbm, left_hbm, right_hbm, out_ref,
    left, right, half, wave, pown, psend, precv, rsend, rrecv, mid, msum, acc, phi, diag, weight, csum,
    sc_src, sc_d, sc_own, sc_recv, pairs_in, tab_v, tab,
    lsem, g1s, g1r, g2s, g2r, g3s, g3r, fws, fwr, pss, psr, rss, rsr, mss, msr, dss, dsr, scs, scr, xs, xr, outs, outr, planes,
):
    x, c, y, z = position()
    me = lax.axis_index("ops")
    sec = z * 4 + y
    mine = sec * 4 + x
    rows = pl.ds(c * H, H)
    sibling = (x * 2 + 1 - c, sec)

    loads = [
        pltpu.make_async_copy(source_hbm, pairs_in.at[pl.ds(0, 1)], lsem.at[0]),
        pltpu.make_async_copy(target_hbm, pairs_in.at[pl.ds(1, 1)], lsem.at[1]),
        pltpu.make_async_copy(psi_hbm.at[:, rows], phi, lsem.at[2]),
        pltpu.make_async_copy(diag_hbm.at[:, rows], diag, lsem.at[3]),
        pltpu.make_async_copy(left_hbm, left, lsem.at[4]),
        pltpu.make_async_copy(right_hbm, right.at[pl.ds(0, PAIRS)], lsem.at[5]),
    ]
    for load in loads:
        load.start()

    def chip(k):
        q = place_of(k)
        return chip_at(lax.rem(q, 4), lax.rem(q // 4, 4), q // 16)

    def chip_at(dx, dy, dz):
        return (lax.rem(x + dx, 4) * 2 + c, lax.rem(z + dz, 4) * 4 + lax.rem(y + dy, 4))

    def place(first, second):
        dy = jnp.where(c == 0, first, second)
        dz = jnp.where(c == 0, second, first)
        return lax.rem(z + dz + 4, 4) * 4 + lax.rem(y + dy + 4, 4)

    barrier = pltpu.get_barrier_semaphore()

    for j in range(1, 4):
        for to in (chip_at(j, 0, 0), chip_at(0, j, 0), chip_at(0, 0, j)):
            pl.semaphore_signal(barrier, inc=1, device_id=to, device_id_type=MESH)
    pl.semaphore_signal(barrier, inc=1, device_id=sibling, device_id_type=MESH)

    loads[2].wait()
    wave[pl.ds(sec * 4, 4), rows, :] = phi[...].astype(jnp.bfloat16)
    pl.semaphore_wait(barrier, 10)

    def remote(src, dst, s, r, to):
        return pltpu.make_async_remote_copy(
            src_ref=src, dst_ref=dst, send_sem=s, recv_sem=r, device_id=to, device_id_type=MESH
        )

    def sectors(at):
        return wave.at[pl.ds(at * 4, 4), rows]

    def two_sectors(at):
        return wave.at[pl.ds(at * 4 + 2 * lax.rem(x, 2), 2), rows]

    def first_copy(j):
        return remote(sectors(sec), sectors(sec), g1s.at[j], g1r.at[j], (me, place(j, 0)))

    def second_copy(j, m):
        block = two_sectors(place(-j, 0)) if j in SHARED else sectors(place(-j, 0))
        n = j * 4 + m
        return remote(block, block, g2s.at[n], g2r.at[n], (me, place(0, m)))

    def share_copy(j, m):
        block = two_sectors(place(-j, -m))
        n = j * 4 + m
        to = lax.rem(x + 3 + 2 * lax.rem(x + j + m + 1, 2), 4) * 2 + c
        return remote(block, block, g3s.at[n], g3r.at[n], (to, sec))

    def forward_copy(j, m):
        block = sectors(place(-j, -m))
        n = j * 4 + m
        return remote(block, block, fws.at[n], fwr.at[n], sibling)

    def partial_copy(b):
        return remote(psend.at[b], precv.at[b], pss.at[b], psr.at[b], sibling)

    def line_sum_copy(g, kk):
        k = g * 4 + kk
        axis = lax.rem(g, 3)
        to = chip_at(*(jnp.where(axis == n, offset(kk), 0) for n in range(3)))
        return remote(rsend.at[k], rrecv.at[k], rss.at[k], rsr.at[k], to)

    def plane_sum_copy(g):
        return remote(mid.at[g], msum.at[g], mss.at[g], msr.at[g], chip(g * 4 + 3))

    def sum_copy(k):
        return remote(rsend.at[k], rrecv.at[k], rss.at[k], rsr.at[k], chip(k))

    def scalar_copy(k):
        return remote(sc_own, sc_recv.at[mine], scs.at[k], scr.at[k], chip(k))

    def line_copy(j):
        to = (lax.rem(x + j, 4) * 2 + c, sec)
        return remote(acc, csum.at[x], xs.at[j], xr.at[j], to)

    def left_products(n):
        picked = wave[tab[1, n]]
        half[n] = jnp.dot(left[tab[0, n]], picked, preferred_element_type=jnp.float32).astype(
            jnp.bfloat16
        )

    def slot(table, k, r):
        return tab[table + k // 32, lax.rem(k, 32) * MOST + r]

    def right_products(h):
        for i in range(EACH):
            k = h * EACH + i
            total = None
            for r in range(0, MOST, 2):
                a = jnp.concatenate([half[slot(2, k, r)], half[slot(2, k, r + 1)]], axis=1)
                w = jnp.concatenate([right[slot(4, k, r)], right[slot(4, k, r + 1)]], axis=1)
                term = lax.dot_general(
                    a, w, (((1,), (1,)), ((), ())), preferred_element_type=jnp.float32
                )
                total = term if total is None else total + term
            low, high = total[:H], total[H:]
            pown[h, i] = jnp.where(c == 0, low, high)
            psend[h, i] = jnp.where(c == 0, high, low)
        partial_copy(h).start()

    def send_lines(h):
        partial_copy(h).wait()
        for i in range(EACH):
            both = pown[h, i] + precv[h, i]
            g, kk = 2 * h + i // 4, i % 4
            if kk == 3:
                mid[g] = both
            else:
                rsend[g * 4 + kk] = both.astype(jnp.bfloat16)
                line_sum_copy(g, kk).start()

    def sum_lines(h):
        for n in range(2):
            g = 2 * h + n
            for kk in range(3):
                line_sum_copy(g, kk).wait_recv()
            got = [rrecv[g * 4 + kk].astype(jnp.float32) for kk in range(3)]
            mid[g] = (mid[g] + got[0]) + (got[1] + got[2])
            plane_sum_copy(g).start()

    def send_straight(h):
        partial_copy(h).wait()
        for i in range(EACH):
            both = pown[h, i] + precv[h, i]
            if isinstance(h, int) and h == TURNS - 1 and i == EACH - 1:
                acc[...] = both
            else:
                rsend[h * EACH + i] = both.astype(jnp.bfloat16)
                sum_copy(h * EACH + i).start()

    to_scalar = pltpu.make_async_copy(tab_v, tab, lsem.at[6])

    def prepare():
        right[PAIRS] = jnp.zeros((B, B), jnp.bfloat16)
        half[PAIRS] = jnp.zeros((B, B), jnp.bfloat16)
        loads[0].wait()
        loads[1].wait()
        tab_v[...] = jnp.zeros((8, B), jnp.int32)
        for n, row in enumerate(pair_tables(pairs_in[0:1, :], pairs_in[1:2, :], x, y, z)):
            tab_v[n : n + 1, :] = row
        to_scalar.start()
        loads[3].wait()
        weight[...] = 1.0 / (diag[...] + 1.0)

    def scalars_sent(n, carry):
        for m in range(9):
            scalar_copy(n * 9 + m).wait_send()
        return carry

    def step(t, theta_before):
        far = (2, 1, 3)
        near = (1, 3, 2)
        for j in far:
            first_copy(j).start()
        for m in far:
            second_copy(0, m).start()
        forward_copy(0, 0).start()

        @pl.when(t == 0)
        def _():
            prepare()

        @pl.when(t > 0)
        def _():
            lax.fori_loop(0, 7, scalars_sent, 0)

        for j in near:
            first_copy(j).wait_recv()
            for m in far:
                second_copy(j, m).start()
            forward_copy(j, 0).start()
        for j in SHARED:
            for m in near:
                second_copy(j, m).wait_recv()
                share_copy(j, m).start()
        for j in WHOLE:
            for m in near:
                second_copy(j, m).wait_recv()
                forward_copy(j, m).start()
        for j in SHARED:
            for m in near:
                share_copy(j, m).wait_recv()
                forward_copy(j, m).start()
        for j in (0, *near):
            for m in (0, *near):
                forward_copy(j, m).wait_recv()

        @pl.when(t == 0)
        def _():
            for j in range(1, 4):
                pl.semaphore_signal(planes, inc=1, device_id=chip_at(j, 0, 0), device_id_type=MESH)
            to_scalar.wait()
            loads[4].wait()
            loads[5].wait()

        def early(h, carry):
            right_products(h)
            for n in range(32):
                left_products((h + 1) * 32 + n)
            return carry

        def middle(h, carry):
            right_products(h)
            send_lines(h - 2)
            return carry

        def late(h, carry):
            right_products(h)
            send_straight(h - 2)
            return carry

        for n in range(32):
            left_products(n)
        lax.fori_loop(0, 3, early, 0)
        send_lines(0)
        lax.fori_loop(3, 6, middle, 0)

        @pl.when(t == 0)
        def _():
            pl.semaphore_wait(planes, 3)

        lax.fori_loop(6, TURNS, late, 0)
        sum_lines(0)
        send_straight(TURNS - 2)
        sum_lines(1)
        send_straight(TURNS - 1)
        sum_lines(2)
        sum_lines(3)

        for j in (0, *near):
            if j:
                first_copy(j).wait_send()
            for m in (0, *near):
                if m:
                    second_copy(j, m).wait_send()
                    if j in SHARED:
                        share_copy(j, m).wait_send()
                forward_copy(j, m).wait_send()

        def collect(n, carry):
            got = []
            for m in range(8):
                k = GROUPS * 4 + n * 8 + m
                sum_copy(k).wait_recv()
                got.append(rrecv[k].astype(jnp.float32))
            pairs = [got[m] + got[m + 1] for m in range(0, 8, 2)]
            acc[...] += (pairs[0] + pairs[1]) + (pairs[2] + pairs[3])
            return carry

        lax.fori_loop(0, 3, collect, 0)
        total = acc[...]
        for k in range(NSEC - 8, NSEC - 1):
            sum_copy(k).wait_recv()
            total += rrecv[k].astype(jnp.float32)
        for g in range(GROUPS):
            plane_sum_copy(g).wait_recv()
            total += msum[g]
        acc[...] = total
        for j in range(1, 4):
            line_copy(j).start()

        now = phi[x]
        csum[x] = total
        sigma = diag[x] * now + total
        ua = now * weight[x]
        fa = now - (sigma - theta_before * now) * weight[x]
        lane = lax.broadcasted_iota(jnp.int32, (1, B), 1)
        row = jnp.zeros((1, B), jnp.float32)
        for j, terms in enumerate((now * sigma, now * now, fa * fa, fa * ua, ua * ua)):
            value = jnp.sum(jnp.sum(terms, axis=0, keepdims=True), axis=1, keepdims=True)
            row = jnp.where(lane == j, value, row)
        sc_src[...] = row
        swap = remote(sc_src, sc_d, dss.at[0], dsr.at[0], sibling)
        swap.start()
        swap.wait()
        sc_own[...] = row + sc_d[...]

        def send_scalars(n, carry):
            for m in range(9):
                scalar_copy(n * 9 + m).start()
            return carry

        def wait_scalars(n, carry):
            for m in range(9):
                scalar_copy(n * 9 + m).wait_recv()
            return carry

        lax.fori_loop(0, 7, send_scalars, 0)
        sc_recv[mine] = sc_own[...]
        for g in range(GROUPS):
            for kk in range(3):
                line_sum_copy(g, kk).wait_send()
            plane_sum_copy(g).wait_send()
        for k in range(GROUPS * 4, NSEC - 1):
            sum_copy(k).wait_send()
        lax.fori_loop(0, 7, wait_scalars, 0)
        sums = jnp.sum(sc_recv[...], axis=0)
        theta = sums[:, 0:1] / sums[:, 1:2]
        delta = theta - theta_before
        squares = sums[:, 2:3] + delta * (2.0 * sums[:, 3:4] + delta * sums[:, 4:5])
        scale = 1.0 / jnp.sqrt(squares / float(NSEC * B * B) + 1e-06)
        for j in range(1, 4):
            line_copy(j).wait()
        for j in range(4):
            now = phi[j]
            fresh = now - (diag[j] * now + csum[j] - theta * now) * weight[j]
            new = fresh * scale
            phi[j] = new
            wave[sec * 4 + j, rows, :] = new.astype(jnp.bfloat16)
        return theta

    lax.fori_loop(0, ITERS, step, jnp.zeros((1, 1), jnp.float32))
    lax.fori_loop(0, 7, scalars_sent, 0)

    out_ref[:, rows, :] = phi[...]
    last = remote(phi, out_ref.at[:, rows], outs.at[0], outr.at[0], sibling)
    last.start()
    last.wait()


def shards(psi, diag_part, left_ops, right_ops, source_sec, target_sec):
    vmem = pl.BlockSpec(memory_space=pltpu.VMEM)
    hbm = pl.BlockSpec(memory_space=pl.ANY)
    f32, bf16 = jnp.float32, jnp.bfloat16
    dma = pltpu.SemaphoreType.DMA
    quarter = pltpu.VMEM((4, H, B), f32)
    line = pltpu.VMEM((1, B), f32)
    partial = pltpu.VMEM((TURNS, EACH, H, B), f32)
    packed = pltpu.VMEM((NSEC, H, B), bf16)
    return pl.pallas_call(
        kernel,
        out_shape=jax.ShapeDtypeStruct((4, B, B), f32),
        in_specs=[hbm] * 6,
        out_specs=vmem,
        scratch_shapes=[
            pltpu.VMEM((PAIRS, B, B), bf16),
            pltpu.VMEM((PAIRS + 1, B, B), bf16),
            pltpu.VMEM((PAIRS + 1, B, B), bf16),
            pltpu.VMEM((NSEC, B, B), bf16),
            partial,
            partial,
            partial,
            packed,
            packed,
            pltpu.VMEM((GROUPS, H, B), f32),
            pltpu.VMEM((GROUPS, H, B), f32),
            pltpu.VMEM((H, B), f32),
            quarter,
            quarter,
            quarter,
            quarter,
            line,
            line,
            line,
            pltpu.VMEM((NSEC, 1, B), f32),
            pltpu.VMEM((8, B), jnp.int32),
            pltpu.VMEM((8, B), jnp.int32),
            pltpu.SMEM((8, B), jnp.int32),
            dma((7,)),
            dma((4,)),
            dma((4,)),
            dma((16,)),
            dma((16,)),
            dma((16,)),
            dma((16,)),
            dma((16,)),
            dma((16,)),
            dma((16,)),
            dma((16,)),
            dma((NSEC,)),
            dma((NSEC,)),
            dma((GROUPS,)),
            dma((GROUPS,)),
            dma((1,)),
            dma((1,)),
            dma((NSEC,)),
            dma((NSEC,)),
            dma((4,)),
            dma((4,)),
            dma((1,)),
            dma((1,)),
            pltpu.SemaphoreType.REGULAR,
        ],
        compiler_params=pltpu.CompilerParams(
            collective_id=0, has_side_effects=True, vmem_limit_bytes=62 << 20
        ),
        cost_estimate=pl.CostEstimate(
            flops=ITERS * PAIRS * 4 * B * B * B, bytes_accessed=9 << 20, transcendentals=0
        ),
        name="davidson",
    )(
        source_sec.reshape(1, PAIRS), target_sec.reshape(1, PAIRS), psi, diag_part, left_ops,
        right_ops,
    )


def solution(mesh):
    placed = (
        P("sec", None, None),
        P("sec", None, None),
        P(("ops", "sec"), None, None),
        P(("ops", "sec"), None, None),
        P(("ops", "sec")),
        P(("ops", "sec"), None),
    )
    return jax.shard_map(
        shards, mesh=mesh, in_specs=placed, out_specs=P("sec", None, None), check_vma=False
    )
```

```python
import jax
import jax.numpy as jnp
from jax import lax
from jax.experimental import pallas as pl
from jax.experimental.pallas import tpu as pltpu
from jax.sharding import PartitionSpec as P

ITERS = 3
MOST = 4
TURNS, EACH = 8, 8
GROUPS = 8
B = 128
H = 64
PAIRS = 128
NSEC = 64
MESH = pl.DeviceIdType.MESH


ORDER = [
    38, 37, 39, 36, 26, 22, 30, 18, 41, 25, 57, 9, 46, 45, 47, 44,
    58, 54, 62, 50, 43, 27, 59, 11, 34, 33, 35, 32, 10, 6, 14, 2,
    42, 40, 21, 63, 23, 61, 29, 55, 31, 53, 24, 56, 17, 51, 5, 15,
    19, 49, 7, 13, 20, 60, 28, 52, 8, 1, 3, 16, 48, 4, 12, 0,
]
WORDS = [
    sum(place * NSEC**n for n, place in enumerate(ORDER[at : at + 5])) for at in range(0, NSEC, 5)
]


def offset(kk):
    return (2, 1, 3, 0)[kk]


def place_of(k):
    word = jnp.int32(WORDS[0])
    for n in range(1, len(WORDS)):
        word = jnp.where(k // 5 == n, jnp.int32(WORDS[n]), word)
    scale = jnp.int32(1)
    for n in range(1, 5):
        scale = jnp.where(lax.rem(k, 5) == n, jnp.int32(NSEC**n), scale)
    return lax.rem(word // scale, NSEC)


def position():
    o, i = lax.axis_index("ops"), lax.axis_index("sec")
    return o // 2, lax.rem(o, 2), lax.rem(i, 4), i // 4


def column(row):
    return jnp.broadcast_to(row, (B, B)).T


def pair_tables(source, target, x, y, z):
    ids = lax.broadcasted_iota(jnp.int32, (B, B), 1)
    down = lax.broadcasted_iota(jnp.int32, (B, B), 0)
    part = target // 4
    dx = lax.rem(lax.rem(target, 4) - x + 4, 4)
    dy = lax.rem(lax.rem(part, 4) - y + 4, 4)
    dz = lax.rem(part // 4 - z + 4, 4)
    seen = dx + 4 * dy + 16 * dz
    key = jnp.zeros_like(seen)
    for n, at in enumerate(ORDER):
        key = jnp.where(seen == at, n, key)
    other = column(key)
    before = (other == key) & (down < ids)

    def count(mask):
        return jnp.sum(jnp.where(mask, 1, 0), axis=0, keepdims=True)

    rank = count(before)
    place = count((other < key) | before)
    place_col = column(place)
    slot_col = column(key * MOST + rank)
    at = place_col == ids

    def pick(mask, values, empty):
        return empty + jnp.sum(jnp.where(mask, values - empty, 0), axis=0, keepdims=True)

    rows = [pick(at, down, 0), pick(at, column(source), 0)]
    for values in (place_col, down):
        for n in range(2):
            rows.append(pick(slot_col == ids + n * B, values, PAIRS))
    return rows


def kernel(
    source_hbm, target_hbm, psi_hbm, diag_hbm, left_hbm, right_hbm, out_ref,
    left, right, half, wave, pown, psend, precv, rsend, rrecv, mid, msum, acc, phi, diag, weight, csum,
    sc_src, sc_d, sc_own, sc_recv, pairs_in, tab_v, tab,
    lsem, g1s, g1r, g2s, g2r, fws, fwr, pss, psr, rss, rsr, mss, msr, dss, dsr, scs, scr, xs, xr, outs, outr, planes,
):
    x, c, y, z = position()
    me = lax.axis_index("ops")
    sec = z * 4 + y
    mine = sec * 4 + x
    rows = pl.ds(c * H, H)
    sibling = (x * 2 + 1 - c, sec)

    loads = [
        pltpu.make_async_copy(source_hbm, pairs_in.at[pl.ds(0, 1)], lsem.at[0]),
        pltpu.make_async_copy(target_hbm, pairs_in.at[pl.ds(1, 1)], lsem.at[1]),
        pltpu.make_async_copy(psi_hbm.at[:, rows], phi, lsem.at[2]),
        pltpu.make_async_copy(diag_hbm.at[:, rows], diag, lsem.at[3]),
        pltpu.make_async_copy(left_hbm, left, lsem.at[4]),
        pltpu.make_async_copy(right_hbm, right.at[pl.ds(0, PAIRS)], lsem.at[5]),
    ]
    for load in loads:
        load.start()

    def chip(k):
        q = place_of(k)
        return chip_at(lax.rem(q, 4), lax.rem(q // 4, 4), q // 16)

    def chip_at(dx, dy, dz):
        return (lax.rem(x + dx, 4) * 2 + c, lax.rem(z + dz, 4) * 4 + lax.rem(y + dy, 4))

    def place(first, second):
        dy = jnp.where(c == 0, first, second)
        dz = jnp.where(c == 0, second, first)
        return lax.rem(z + dz + 4, 4) * 4 + lax.rem(y + dy + 4, 4)

    barrier = pltpu.get_barrier_semaphore()

    for j in range(1, 4):
        for to in (chip_at(j, 0, 0), chip_at(0, j, 0), chip_at(0, 0, j)):
            pl.semaphore_signal(barrier, inc=1, device_id=to, device_id_type=MESH)
    pl.semaphore_signal(barrier, inc=1, device_id=sibling, device_id_type=MESH)

    loads[2].wait()
    wave[pl.ds(sec * 4, 4), rows, :] = phi[...].astype(jnp.bfloat16)
    pl.semaphore_wait(barrier, 10)

    def remote(src, dst, s, r, to):
        return pltpu.make_async_remote_copy(
            src_ref=src, dst_ref=dst, send_sem=s, recv_sem=r, device_id=to, device_id_type=MESH
        )

    def sectors(at):
        return wave.at[pl.ds(at * 4, 4), rows]

    def first_copy(j):
        return remote(sectors(sec), sectors(sec), g1s.at[j], g1r.at[j], (me, place(j, 0)))

    def second_copy(j, m):
        block = sectors(place(-j, 0))
        n = j * 4 + m
        return remote(block, block, g2s.at[n], g2r.at[n], (me, place(0, m)))

    def forward_copy(j, m):
        block = sectors(place(-j, -m))
        n = j * 4 + m
        return remote(block, block, fws.at[n], fwr.at[n], sibling)

    def partial_copy(h, part):
        at, four = 2 * h + part, pl.ds(4 * part, 4)
        return remote(psend.at[h, four], precv.at[h, four], pss.at[at], psr.at[at], sibling)

    def line_sum_copy(g, kk):
        k = g * 4 + kk
        axis = lax.rem(g, 3)
        to = chip_at(*(jnp.where(axis == n, offset(kk), 0) for n in range(3)))
        return remote(rsend.at[k], rrecv.at[k], rss.at[k], rsr.at[k], to)

    def plane_sum_copy(g):
        return remote(mid.at[g], msum.at[g], mss.at[g], msr.at[g], chip(g * 4 + 3))

    def sum_copy(k):
        return remote(rsend.at[k], rrecv.at[k], rss.at[k], rsr.at[k], chip(k))

    def scalar_copy(k):
        return remote(sc_own, sc_recv.at[mine], scs.at[k], scr.at[k], chip(k))

    def line_copy(j):
        to = (lax.rem(x + j, 4) * 2 + c, sec)
        return remote(acc, csum.at[x], xs.at[j], xr.at[j], to)

    def left_products(n):
        picked = wave[tab[1, n]]
        half[n] = jnp.dot(left[tab[0, n]], picked, preferred_element_type=jnp.float32).astype(
            jnp.bfloat16
        )

    def slot(table, k, r):
        return tab[table + k // 32, lax.rem(k, 32) * MOST + r]

    def right_products(h):
        for i in range(EACH):
            k = h * EACH + i
            total = None
            for r in range(0, MOST, 2):
                a = jnp.concatenate([half[slot(2, k, r)], half[slot(2, k, r + 1)]], axis=1)
                w = jnp.concatenate([right[slot(4, k, r)], right[slot(4, k, r + 1)]], axis=1)
                term = lax.dot_general(
                    a, w, (((1,), (1,)), ((), ())), preferred_element_type=jnp.float32
                )
                total = term if total is None else total + term
            low, high = total[:H], total[H:]
            pown[h, i] = jnp.where(c == 0, low, high)
            psend[h, i] = jnp.where(c == 0, high, low)
            if i % 4 == 3:
                partial_copy(h, i // 4).start()

    def send_lines(h):
        for i in range(EACH):
            if i % 4 == 0:
                partial_copy(h, i // 4).wait()
            both = pown[h, i] + precv[h, i]
            g, kk = 2 * h + i // 4, i % 4
            if kk == 3:
                mid[g] = both
            else:
                rsend[g * 4 + kk] = both.astype(jnp.bfloat16)
                line_sum_copy(g, kk).start()

    def sum_lines(h):
        for n in range(2):
            g = 2 * h + n
            for kk in range(3):
                line_sum_copy(g, kk).wait_recv()
            got = [rrecv[g * 4 + kk].astype(jnp.float32) for kk in range(3)]
            mid[g] = (mid[g] + got[0]) + (got[1] + got[2])
            plane_sum_copy(g).start()

    def send_straight(h):
        for i in range(EACH):
            if i % 4 == 0:
                partial_copy(h, i // 4).wait()
            both = pown[h, i] + precv[h, i]
            if isinstance(h, int) and h == TURNS - 1 and i == EACH - 1:
                acc[...] = both
            else:
                rsend[h * EACH + i] = both.astype(jnp.bfloat16)
                sum_copy(h * EACH + i).start()

    def prepare():
        right[PAIRS] = jnp.zeros((B, B), jnp.bfloat16)
        half[PAIRS] = jnp.zeros((B, B), jnp.bfloat16)
        loads[0].wait()
        loads[1].wait()
        tab_v[...] = jnp.zeros((8, B), jnp.int32)
        for n, row in enumerate(pair_tables(pairs_in[0:1, :], pairs_in[1:2, :], x, y, z)):
            tab_v[n : n + 1, :] = row
        to_scalar = pltpu.make_async_copy(tab_v, tab, lsem.at[6])
        to_scalar.start()
        loads[3].wait()
        weight[...] = 1.0 / (diag[...] + 1.0)
        to_scalar.wait()

    def scalars_sent(n, carry):
        for m in range(9):
            scalar_copy(n * 9 + m).wait_send()
        return carry

    def step(t, theta_before):
        far = (2, 1, 3)
        near = (1, 3, 2)
        for j in far:
            first_copy(j).start()
        for m in far:
            second_copy(0, m).start()
        forward_copy(0, 0).start()

        @pl.when(t == 0)
        def _():
            prepare()

        @pl.when(t > 0)
        def _():
            lax.fori_loop(0, 7, scalars_sent, 0)

        for j in near:
            first_copy(j).wait_recv()
            for m in far:
                second_copy(j, m).start()
            forward_copy(j, 0).start()
        for j in (0, *near):
            for m in near:
                second_copy(j, m).wait_recv()
                forward_copy(j, m).start()
        for j in (0, *near):
            for m in (0, *near):
                forward_copy(j, m).wait_recv()

        @pl.when(t == 0)
        def _():
            for j in range(1, 4):
                pl.semaphore_signal(planes, inc=1, device_id=chip_at(j, 0, 0), device_id_type=MESH)
            loads[4].wait()
            loads[5].wait()

        def early(h, carry):
            right_products(h)
            for n in range(32):
                left_products((h + 1) * 32 + n)
            return carry

        def middle(h, carry):
            right_products(h)
            send_lines(h - 2)
            return carry

        def late(h, carry):
            right_products(h)
            send_straight(h - 2)
            return carry

        for n in range(32):
            left_products(n)
        lax.fori_loop(0, 3, early, 0)
        send_lines(0)
        lax.fori_loop(3, 6, middle, 0)

        @pl.when(t == 0)
        def _():
            pl.semaphore_wait(planes, 3)

        lax.fori_loop(6, TURNS, late, 0)
        sum_lines(0)
        send_straight(TURNS - 2)
        sum_lines(1)
        send_straight(TURNS - 1)
        sum_lines(2)
        sum_lines(3)

        for j in (0, *near):
            if j:
                first_copy(j).wait_send()
            for m in (0, *near):
                if m:
                    second_copy(j, m).wait_send()
                forward_copy(j, m).wait_send()

        def collect(n, carry):
            got = []
            for m in range(8):
                k = GROUPS * 4 + n * 8 + m
                sum_copy(k).wait_recv()
                got.append(rrecv[k].astype(jnp.float32))
            pairs = [got[m] + got[m + 1] for m in range(0, 8, 2)]
            acc[...] += (pairs[0] + pairs[1]) + (pairs[2] + pairs[3])
            return carry

        lax.fori_loop(0, 3, collect, 0)
        total = acc[...]
        for k in range(NSEC - 8, NSEC - 1):
            sum_copy(k).wait_recv()
            total += rrecv[k].astype(jnp.float32)
        for g in range(GROUPS):
            plane_sum_copy(g).wait_recv()
            total += msum[g]
        acc[...] = total
        for j in range(1, 4):
            line_copy(j).start()

        now = phi[x]
        csum[x] = total
        sigma = diag[x] * now + total
        ua = now * weight[x]
        fa = now - (sigma - theta_before * now) * weight[x]
        lane = lax.broadcasted_iota(jnp.int32, (1, B), 1)
        row = jnp.zeros((1, B), jnp.float32)
        for j, terms in enumerate((now * sigma, now * now, fa * fa, fa * ua, ua * ua)):
            value = jnp.sum(jnp.sum(terms, axis=0, keepdims=True), axis=1, keepdims=True)
            row = jnp.where(lane == j, value, row)
        sc_src[...] = row
        swap = remote(sc_src, sc_d, dss.at[0], dsr.at[0], sibling)
        swap.start()
        swap.wait()
        sc_own[...] = row + sc_d[...]

        def send_scalars(n, carry):
            for m in range(9):
                scalar_copy(n * 9 + m).start()
            return carry

        def wait_scalars(n, carry):
            for m in range(9):
                scalar_copy(n * 9 + m).wait_recv()
            return carry

        lax.fori_loop(0, 7, send_scalars, 0)
        sc_recv[mine] = sc_own[...]
        for g in range(GROUPS):
            for kk in range(3):
                line_sum_copy(g, kk).wait_send()
            plane_sum_copy(g).wait_send()
        for k in range(GROUPS * 4, NSEC - 1):
            sum_copy(k).wait_send()
        lax.fori_loop(0, 7, wait_scalars, 0)
        sums = jnp.sum(sc_recv[...], axis=0)
        theta = sums[:, 0:1] / sums[:, 1:2]
        delta = theta - theta_before
        squares = sums[:, 2:3] + delta * (2.0 * sums[:, 3:4] + delta * sums[:, 4:5])
        scale = 1.0 / jnp.sqrt(squares / float(NSEC * B * B) + 1e-06)
        for j in range(1, 4):
            line_copy(j).wait()
        for j in range(4):
            now = phi[j]
            fresh = now - (diag[j] * now + csum[j] - theta * now) * weight[j]
            new = fresh * scale
            phi[j] = new
            wave[sec * 4 + j, rows, :] = new.astype(jnp.bfloat16)
        return theta

    lax.fori_loop(0, ITERS, step, jnp.zeros((1, 1), jnp.float32))
    lax.fori_loop(0, 7, scalars_sent, 0)

    out_ref[:, rows, :] = phi[...]
    last = remote(phi, out_ref.at[:, rows], outs.at[0], outr.at[0], sibling)
    last.start()
    last.wait()


def shards(psi, diag_part, left_ops, right_ops, source_sec, target_sec):
    vmem = pl.BlockSpec(memory_space=pltpu.VMEM)
    hbm = pl.BlockSpec(memory_space=pl.ANY)
    f32, bf16 = jnp.float32, jnp.bfloat16
    dma = pltpu.SemaphoreType.DMA
    quarter = pltpu.VMEM((4, H, B), f32)
    line = pltpu.VMEM((1, B), f32)
    partial = pltpu.VMEM((TURNS, EACH, H, B), f32)
    packed = pltpu.VMEM((NSEC, H, B), bf16)
    return pl.pallas_call(
        kernel,
        out_shape=jax.ShapeDtypeStruct((4, B, B), f32),
        in_specs=[hbm] * 6,
        out_specs=vmem,
        scratch_shapes=[
            pltpu.VMEM((PAIRS, B, B), bf16),
            pltpu.VMEM((PAIRS + 1, B, B), bf16),
            pltpu.VMEM((PAIRS + 1, B, B), bf16),
            pltpu.VMEM((NSEC, B, B), bf16),
            partial,
            partial,
            partial,
            packed,
            packed,
            pltpu.VMEM((GROUPS, H, B), f32),
            pltpu.VMEM((GROUPS, H, B), f32),
            pltpu.VMEM((H, B), f32),
            quarter,
            quarter,
            quarter,
            quarter,
            line,
            line,
            line,
            pltpu.VMEM((NSEC, 1, B), f32),
            pltpu.VMEM((8, B), jnp.int32),
            pltpu.VMEM((8, B), jnp.int32),
            pltpu.SMEM((8, B), jnp.int32),
            dma((7,)),
            dma((4,)),
            dma((4,)),
            dma((16,)),
            dma((16,)),
            dma((16,)),
            dma((16,)),
            dma((16,)),
            dma((16,)),
            dma((NSEC,)),
            dma((NSEC,)),
            dma((GROUPS,)),
            dma((GROUPS,)),
            dma((1,)),
            dma((1,)),
            dma((NSEC,)),
            dma((NSEC,)),
            dma((4,)),
            dma((4,)),
            dma((1,)),
            dma((1,)),
            pltpu.SemaphoreType.REGULAR,
        ],
        compiler_params=pltpu.CompilerParams(
            collective_id=0, has_side_effects=True, vmem_limit_bytes=62 << 20
        ),
        cost_estimate=pl.CostEstimate(
            flops=ITERS * PAIRS * 4 * B * B * B, bytes_accessed=9 << 20, transcendentals=0
        ),
        name="davidson",
    )(
        source_sec.reshape(1, PAIRS), target_sec.reshape(1, PAIRS), psi, diag_part, left_ops,
        right_ops,
    )


def solution(mesh):
    placed = (
        P("sec", None, None),
        P("sec", None, None),
        P(("ops", "sec"), None, None),
        P(("ops", "sec"), None, None),
        P(("ops", "sec")),
        P(("ops", "sec"), None),
    )
    return jax.shard_map(
        shards, mesh=mesh, in_specs=placed, out_specs=P("sec", None, None), check_vma=False
    )
```
